256 devices in a mesh: ctx: 32 (over z, y), ch: 8 (over x, core).
Axes of the slice: x: 4, y: 4, z: 8, core: 2. Of those that a mesh axis runs over, the one named last changes fastest.
Arguments:
- queries: bfloat16 [8192, 4096], P('ctx', 'ch'), may hold values from -6 to 6
- keys: bfloat16 [8192, 4096], P('ctx', 'ch'), may hold values from -6 to 6
- values: bfloat16 [8192, 4096], P('ctx', 'ch'), may hold values from -6 to 6
- long_filter: float32 [8192, 4096], P('ctx', 'ch'), may hold values from -1.05 to 1.05
- short_filters: float32 [3, 3, 4096], P(None, None, 'ch'), may hold values from -3.6 to 3.6
- skip: float32 [4096], P('ch'), may hold values from -1 to 1
- w_out: bfloat16 [4096, 8192], P('ch'), may hold values from -0.09375 to 0.09375
- d_out: bfloat16 [8192, 8192], P('ctx', 'ch'), may hold values from -6 to 6
Outputs:
- d_queries: bfloat16 [8192, 4096], P('ctx', 'ch')
- d_keys: bfloat16 [8192, 4096], P('ctx', 'ch')
- d_values: bfloat16 [8192, 4096], P('ctx', 'ch')
- d_long: float32 [8192, 4096], P('ctx', 'ch')
- d_short: float32 [3, 3, 4096], P(None, None, 'ch')
- d_skip: float32 [4096], P('ch')
The draws below stay inside these ranges and needn't reach their ends.
All inputs are finite; a program needn't handle non-finite values.
Results may differ from the reference program's by a relative error of at most 0.0049.
Values may be sent and summed in bfloat16 or wider, within the bound.
No kernel may reach another device: no remote copies, remote signals or barrier semaphores. Data moves between devices by JAX's collectives and lax.ppermute only.
A program may use at most 128 MiB of HBM per device.

```python
import jax
import jax.numpy as jnp
from jax import lax

D = 8192
CHANNELS = 4096
TAPS = 3
LENGTH = 8192


def draw_long_filter(key, part):
    rate_key = jax.random.fold_in(key, 11)
    noise_key = jax.random.fold_in(key, 23)
    low = jnp.log(jnp.float32(1.0) / (4.0 * LENGTH))
    high = jnp.log(jnp.float32(1.0) / 30.0)
    rates = jnp.exp(jax.random.uniform(rate_key, (CHANNELS,), jnp.float32, low, high))
    steps = jnp.arange(LENGTH, dtype=jnp.float32)
    scale = jnp.sqrt(jnp.maximum(2.0 * rates, 1.0 / LENGTH))
    envelope = jnp.exp(-steps[:, None] * rates[None, :]) * scale[None, :]
    noise = jnp.clip(jax.random.normal(noise_key, (LENGTH, CHANNELS), jnp.float32), -4.0, 4.0)
    return (noise * envelope).astype(jnp.float32)


def block_scale(stream_key, dims, shards, smallest, largest):
    factor_of, own = 1.0, jax.random.fold_in(stream_key, 6)
    for axis_at, shards_of in shards:
        steps = jnp.exp(jax.random.uniform(jax.random.fold_in(own, axis_at), (shards_of,), jnp.float32, smallest / len(shards), largest / len(shards)))
        factor_of = factor_of * jnp.repeat(steps, dims[axis_at] // shards_of).reshape([-1 if axis == axis_at else 1 for axis in range(len(dims))])
    return factor_of


def scatter_about(own_key, shape, scale, bound, pieces=(), kind=jnp.bfloat16):
    level = block_scale(own_key, shape, pieces, -0.22, 0.18) if pieces else 1.0
    array = jax.random.normal(own_key, shape, jnp.float32) * scale * level
    return jnp.minimum(jnp.maximum(array, -bound), bound).astype(kind)


def setup_inputs(seed: int = 0) -> dict:
    streams_of = jax.random.split(jax.random.key(seed), 9)
    return {
        "queries": scatter_about(streams_of[0], (LENGTH, CHANNELS), 1.0, 6.0, ((0, 32), (1, 8))),
        "keys": scatter_about(streams_of[1], (LENGTH, CHANNELS), 1.0, 6.0, ((0, 32), (1, 8))),
        "values": scatter_about(streams_of[2], (LENGTH, CHANNELS), 1.0, 6.0, ((0, 32), (1, 8))),
        "long_filter": draw_long_filter(jax.random.fold_in(streams_of[8], 71), 0),
        "short_filters": scatter_about(streams_of[4], (3, TAPS, CHANNELS), 0.6, 3.6, ((2, 8),), jnp.float32),
        "skip": jnp.clip(jax.random.uniform(streams_of[5], (CHANNELS,), jnp.float32, -1.0, 1.0) * block_scale(streams_of[5], (CHANNELS,), ((0, 8),), -0.4, 0.0), -1.0, 1.0),
        "w_out": scatter_about(streams_of[6], (CHANNELS, D), CHANNELS ** -0.5, 0.09375, ((0, 8),)),
        "d_out": scatter_about(streams_of[7], (LENGTH, D), 1.0, 6.0, ((0, 32), (1, 8))),
    }


def short_conv(stream, taps):
    padded = jnp.pad(stream, ((TAPS - 1, 0), (0, 0)))
    result = jnp.zeros(stream.shape, jnp.float32)
    for j in range(TAPS):
        result = result + taps[j][None, :] * padded[TAPS - 1 - j:TAPS - 1 - j + LENGTH]
    return result, padded


def back_conv(grad, taps):
    padded = jnp.pad(grad, ((0, TAPS - 1), (0, 0)))
    result = jnp.zeros(grad.shape, jnp.float32)
    for j in range(TAPS):
        result = result + taps[j][None, :] * padded[j:j + LENGTH]
    return result


def reference(queries, keys, values, long_filter, short_filters, skip, w_out, d_out):
    streams = [queries.astype(jnp.float32), keys.astype(jnp.float32), values.astype(jnp.float32)]
    filtered = []
    padded_in = []
    for s in range(3):
        out_s, pad_s = short_conv(streams[s], short_filters[s])
        filtered.append(out_s)
        padded_in.append(pad_s)
    mixed = filtered[1] * filtered[2]
    grad_o = jnp.dot(d_out, w_out.T, preferred_element_type=jnp.float32).astype(jnp.bfloat16)
    grad_o = lax.optimization_barrier(grad_o).astype(jnp.float32)
    grad_y = grad_o * filtered[0]
    total = 2 * LENGTH
    spec_mixed = jnp.fft.rfft(mixed, n=total, axis=0)
    spec_filter = jnp.fft.rfft(long_filter, n=total, axis=0)
    spec_grad = jnp.fft.rfft(grad_y, n=total, axis=0)
    conv_y = jnp.fft.irfft(spec_mixed * spec_filter, n=total, axis=0)[:LENGTH].astype(jnp.float32)
    conv_back = jnp.fft.irfft(spec_grad * jnp.conj(spec_filter), n=total, axis=0)[:LENGTH].astype(jnp.float32)
    d_long = jnp.fft.irfft(spec_grad * jnp.conj(spec_mixed), n=total, axis=0)[:LENGTH].astype(jnp.float32)
    y_full = conv_y + skip[None, :] * mixed
    grad_mixed = conv_back + skip[None, :] * grad_y
    d_skip = jnp.sum(grad_y * mixed, axis=0)
    grads = [grad_o * y_full, grad_mixed * filtered[2], grad_mixed * filtered[1]]
    short_rows = []
    for s in range(3):
        tap_rows = []
        for j in range(TAPS):
            tap_rows.append(jnp.sum(grads[s] * padded_in[s][TAPS - 1 - j:TAPS - 1 - j + LENGTH], axis=0))
        short_rows.append(jnp.stack(tap_rows))
    d_short = jnp.stack(short_rows)
    d_queries = back_conv(grads[0], short_filters[0]).astype(jnp.bfloat16)
    d_keys = back_conv(grads[1], short_filters[1]).astype(jnp.bfloat16)
    d_values = back_conv(grads[2], short_filters[2]).astype(jnp.bfloat16)
    return (d_queries, d_keys, d_values, d_long, d_short, d_skip)
```

```python
import math

import jax
import jax.numpy as jnp
import numpy as np
from jax import lax
from jax.experimental import pallas as pl
from jax.experimental.pallas import tpu as pltpu
from jax.sharding import Mesh, PartitionSpec as P

F32 = jnp.float32
BF16 = jnp.bfloat16
CTX = ("z", "y")
CH = ("x", "core")
SHARDS = 32
ROWS = 256
GROUP = 16
HALF = 8
WIDTH = 512
LENGTH = SHARDS * ROWS
VMEM_LIMIT = 56 * 1024 * 1024


def halves(table):
    high = table.astype(np.float32).astype(jnp.bfloat16)
    low = (table - high.astype(np.float64)).astype(np.float32).astype(jnp.bfloat16)
    return np.asarray(high), np.asarray(low)


def tables():
    coarse = np.arange(SHARDS)
    angle = 2.0 * math.pi * ((np.outer(4 * coarse + 1, coarse) % (4 * SHARDS)) / (4.0 * SHARDS))
    same = np.eye(HALF)
    spread = np.concatenate([np.kron(np.cos(angle), same), np.kron(-np.sin(angle), same)], axis=0)
    fine = np.arange(ROWS)
    angle = 2.0 * math.pi * ((np.outer(fine, fine) % ROWS) / ROWS)
    cos, sin = np.cos(angle), np.sin(angle)
    turn = np.block([[cos, -sin], [sin, cos]])
    twist = 2.0 * math.pi * np.outer(4 * coarse + 1, fine) / (4.0 * LENGTH)
    twist = np.repeat(np.stack([np.cos(twist), np.sin(twist)]), HALF, axis=1).astype(np.float32)
    return (
        *halves(spread),
        *halves(spread.T / LENGTH),
        *halves(turn),
        *halves(turn.T),
        twist,
    )


def dot(left, right):
    return lax.dot_general(left, right, (((1,), (0,)), ((), ())), preferred_element_type=F32)


def split(value):
    high = value.astype(BF16)
    return high, (value - high.astype(F32)).astype(BF16)


def forward(signal, sh, sl, th, tl, twist):
    parts = signal.astype(F32).reshape(SHARDS, 2, HALF, ROWS)
    rows = SHARDS * HALF
    turned = []
    for g in range(2):
        part = parts[:, g].reshape(rows, ROWS).astype(BF16)
        first = dot(sh[...], part) + dot(sl[...], part)
        real, imag = first[:rows], first[rows:]
        turned.append(
            jnp.concatenate(
                [real * twist[0] + imag * twist[1], imag * twist[0] - real * twist[1]], axis=1
            )
        )
    high, low = split(jnp.concatenate(turned, axis=0))
    return dot(high, th[...]) + dot(low, th[...]) + dot(high, tl[...])


def inverse(real, imag, vh, vl, uh, ul, twist):
    high, low = split(jnp.concatenate([real, imag], axis=1))
    back = dot(high, uh[...]) + dot(low, uh[...]) + dot(high, ul[...])
    rows = SHARDS * HALF
    outs = []
    for g in range(2):
        real = back[g * rows : (g + 1) * rows, :ROWS]
        imag = back[g * rows : (g + 1) * rows, ROWS:]
        high, low = split(
            jnp.concatenate(
                [real * twist[0] - imag * twist[1], imag * twist[0] + real * twist[1]], axis=0
            )
        )
        out = dot(vh[...], high) + dot(vh[...], low) + dot(vl[...], high)
        outs.append(out.reshape(SHARDS, HALF, ROWS))
    return jnp.concatenate(outs, axis=1).astype(BF16)


def conv_kernel(moved, sh, sl, vh, vl, th, tl, uh, ul, twist, spec_mix, spec_fil, out):
    mix = forward(moved[:, 0], sh, sl, th, tl, twist)
    fil = forward(moved[:, 1], sh, sl, th, tl, twist)
    spec_mix[...] = mix
    spec_fil[...] = fil
    mix_re, mix_im = mix[:, :ROWS], mix[:, ROWS:]
    fil_re, fil_im = fil[:, :ROWS], fil[:, ROWS:]
    out[...] = inverse(
        mix_re * fil_re - mix_im * fil_im,
        mix_re * fil_im + mix_im * fil_re,
        vh, vl, uh, ul, twist,
    )


def grad_kernel(moved, spec_mix, spec_fil, sh, sl, vh, vl, th, tl, uh, ul, twist, out):
    grad = forward(moved[...], sh, sl, th, tl, twist)
    grad_re, grad_im = grad[:, :ROWS], grad[:, ROWS:]
    for i, spec in enumerate((spec_fil, spec_mix)):
        re, im = spec[:, :ROWS], spec[:, ROWS:]
        out[:, i] = inverse(
            grad_re * re + grad_im * im, grad_im * re - grad_re * im, vh, vl, uh, ul, twist
        )


def mix_kernel(queries, keys, values, before, short, long_filter, send, filtered, ext):
    for s, stream in enumerate((queries, keys, values)):
        ext[0:8, :] = before[s]
        ext[8 : 8 + ROWS, :] = stream[...].astype(F32)
        total = short[s, 0:1, :] * ext[8 : 8 + ROWS, :]
        for j in (1, 2):
            total = total + short[s, j : j + 1, :] * ext[8 - j : 8 - j + ROWS, :]
        filtered[s] = total
    mixed = filtered[1] * filtered[2]
    send[:, 0] = mixed.T.reshape(SHARDS, GROUP, ROWS).astype(BF16)
    send[:, 1] = long_filter[...].T.reshape(SHARDS, GROUP, ROWS).astype(BF16)


def out_proj_kernel(gathered, w_out, filtered, grad_o, send, total):
    step = pl.program_id(0)

    @pl.when(step == 0)
    def _():
        total[...] = jnp.zeros_like(total)

    total[...] += lax.dot_general(
        gathered[0], w_out[...], (((1,), (1,)), ((), ())), preferred_element_type=F32
    )

    @pl.when(step == pl.num_programs(0) - 1)
    def _():
        rounded = total[...].astype(BF16)
        grad_o[...] = rounded
        grad_y = rounded.astype(F32) * filtered[0]
        send[...] = grad_y.T.reshape(SHARDS, GROUP, ROWS).astype(BF16)


def back_kernel(
    grad_o, filtered, conv_y, conv_back, skip, queries, keys, values, before,
    grads, heads, sums, d_long, ext,
):
    grad = grad_o[...].astype(F32)
    mixed = filtered[1] * filtered[2]
    grad_y = grad * filtered[0]
    time_y = conv_y[...].reshape(WIDTH, ROWS).astype(F32).T
    time_back = conv_back[:, 0].reshape(WIDTH, ROWS).astype(F32).T
    d_long[...] = conv_back[:, 1].reshape(WIDTH, ROWS).astype(F32).T
    grad_mixed = time_back + skip[...] * grad_y
    grads[0, 0:ROWS] = grad * (time_y + skip[...] * mixed)
    grads[1, 0:ROWS] = grad_mixed * filtered[2]
    grads[2, 0:ROWS] = grad_mixed * filtered[1]
    sums[...] = jnp.zeros_like(sums)
    for s, stream in enumerate((queries, keys, values)):
        ext[0:8, :] = before[s]
        ext[8 : 8 + ROWS, :] = stream[...].astype(F32)
        heads[s] = grads[s, 0:8]
        for j in range(3):
            sums[3 * s + j : 3 * s + j + 1, :] = jnp.sum(
                grads[s] * ext[8 - j : 8 - j + ROWS, :], axis=0, keepdims=True
            )
    sums[9:10, :] = jnp.sum(grad_y * mixed, axis=0, keepdims=True)


def taps_kernel(grads, after, short, d_queries, d_keys, d_values, ext):
    for s, out in enumerate((d_queries, d_keys, d_values)):
        ext[0:ROWS, :] = grads[s]
        ext[ROWS : ROWS + 8, :] = after[s]
        total = short[s, 0:1, :] * ext[0:ROWS, :]
        for j in (1, 2):
            total = total + short[s, j : j + 1, :] * ext[j : j + ROWS, :]
        out[...] = total.astype(BF16)


def call(kernel, out_shape, *args, scratch=(), name):
    return pl.pallas_call(
        kernel,
        out_shape=out_shape,
        scratch_shapes=scratch,
        compiler_params=pltpu.CompilerParams(vmem_limit_bytes=VMEM_LIMIT),
        name=name,
    )(*args)


def passed_along(block, distance):
    route = [(i - distance, i) for i in range(SHARDS) if 0 <= i - distance < SHARDS]
    return lax.ppermute(block, CTX, route)


def exchange(blocks):
    return lax.all_to_all(blocks, CTX, split_axis=0, concat_axis=0, tiled=True)


def shape(dims, dtype=F32):
    return jax.ShapeDtypeStruct(dims, dtype)


def per_device(queries, keys, values, long_filter, short, skip, w_out, d_out):
    constants = [jnp.asarray(table) for table in tables()]
    gathered = lax.all_gather(d_out, CH, axis=0, tiled=False)
    tails = jnp.stack([queries[ROWS - 2 :], keys[ROWS - 2 :], values[ROWS - 2 :]])
    before = passed_along(tails, 1).astype(F32)
    before = jnp.concatenate([jnp.zeros((3, 6, WIDTH), F32), before], axis=1)
    extended = pltpu.VMEM((ROWS + 8, WIDTH), F32)
    send, filtered = call(
        mix_kernel,
        (shape((SHARDS, 2, GROUP, ROWS), BF16), shape((3, ROWS, WIDTH))),
        queries, keys, values, before, short, long_filter,
        scratch=(extended,),
        name="mix",
    )
    moved = exchange(send)
    spec = shape((2 * SHARDS * HALF, 2 * ROWS))
    spec_mix, spec_fil, conv_y = call(
        conv_kernel,
        (spec, spec, shape((SHARDS, GROUP, ROWS), BF16)),
        moved, *constants,
        name="conv",
    )
    conv_y = exchange(conv_y)
    steps, depth = gathered.shape[0], gathered.shape[2]
    grad_o, grad_send = pl.pallas_call(
        out_proj_kernel,
        grid=(steps,),
        in_specs=[
            pl.BlockSpec((1, ROWS, depth), lambda i: (i, 0, 0)),
            pl.BlockSpec((WIDTH, depth), lambda i: (0, i)),
            pl.BlockSpec((1, ROWS, WIDTH), lambda i: (0, 0, 0)),
        ],
        out_specs=[
            pl.BlockSpec((ROWS, WIDTH), lambda i: (0, 0)),
            pl.BlockSpec((SHARDS, GROUP, ROWS), lambda i: (0, 0, 0)),
        ],
        out_shape=(shape((ROWS, WIDTH), BF16), shape((SHARDS, GROUP, ROWS), BF16)),
        scratch_shapes=[pltpu.VMEM((ROWS, WIDTH), F32)],
        compiler_params=pltpu.CompilerParams(vmem_limit_bytes=VMEM_LIMIT),
        name="out_proj",
    )(gathered, w_out, filtered)
    grad_moved = exchange(grad_send)
    returned = call(
        grad_kernel,
        shape((SHARDS, 2, GROUP, ROWS), BF16),
        grad_moved, spec_mix, spec_fil, *constants,
        name="grad_conv",
    )
    returned = exchange(returned)
    grads, heads, sums, d_long = call(
        back_kernel,
        (shape((3, ROWS, WIDTH)), shape((3, 8, WIDTH)), shape((16, WIDTH)), shape((ROWS, WIDTH))),
        grad_o, filtered, conv_y, returned, skip[None, :], queries, keys, values, before,
        scratch=(extended,),
        name="back",
    )
    after = passed_along(heads, -1)
    shared = exchange(jnp.broadcast_to(sums.astype(BF16)[None], (SHARDS, 16, WIDTH)))
    totals = jnp.sum(shared.astype(F32), axis=0)
    outs = call(
        taps_kernel,
        (shape((ROWS, WIDTH), BF16),) * 3,
        grads, after, short,
        scratch=(extended,),
        name="taps",
    )
    return (*outs, d_long, totals[:9].reshape(3, 3, WIDTH), totals[9])


def solution(mesh):
    fine_mesh = Mesh(mesh.devices.reshape(8, 4, 4, 2), ("z", "y", "x", "core"))
    block = P(CTX, CH)
    in_specs = (block, block, block, block, P(None, None, CH), P(CH), P(CH, None), block)
    out_specs = (block, block, block, block, P(None, None, CH), P(CH))
    return jax.shard_map(
        per_device, mesh=fine_mesh, in_specs=in_specs, out_specs=out_specs, check_vma=False
    )
```

```python
import functools
import math

import jax
import jax.numpy as jnp
import numpy as np
from jax import lax
from jax.experimental import pallas as pl
from jax.experimental.pallas import tpu as pltpu
from jax.sharding import Mesh, PartitionSpec as P

F32 = jnp.float32
BF16 = jnp.bfloat16
CTX = ("z", "y")
CH = ("x", "core")
SHARDS = 32
ROWS = 256
GROUP = 16
HALF = 8
WIDTH = 512
LENGTH = SHARDS * ROWS
MIB = 1024 * 1024


def halves(table):
    high = table.astype(np.float32).astype(jnp.bfloat16)
    low = (table - high.astype(np.float64)).astype(np.float32).astype(jnp.bfloat16)
    return np.asarray(high), np.asarray(low)


def tables():
    coarse = np.arange(SHARDS)
    angle = 2.0 * math.pi * ((np.outer(4 * coarse + 1, coarse) % (4 * SHARDS)) / (4.0 * SHARDS))
    same = np.eye(HALF)
    spread = np.concatenate([np.kron(np.cos(angle), same), np.kron(-np.sin(angle), same)], axis=0)
    fine = np.arange(ROWS)
    angle = 2.0 * math.pi * ((np.outer(fine, fine) % ROWS) / ROWS)
    cos, sin = np.cos(angle), np.sin(angle)
    turn = np.block([[cos, -sin], [sin, cos]])
    twist = 2.0 * math.pi * np.outer(4 * coarse + 1, fine) / (4.0 * LENGTH)
    twist = np.stack([np.cos(twist), np.sin(twist)])[:, :, None].astype(np.float32)
    return (*halves(spread), *halves(spread.T / LENGTH), *halves(turn), twist)


def dot(left, right):
    return lax.dot_general(left, right, (((1,), (0,)), ((), ())), preferred_element_type=F32)


def split(value):
    high = value.astype(BF16)
    return high, (value - high.astype(F32)).astype(BF16)


def forward(parts, exact, sh, sl, vh, vl, th, tl, twist):
    rows = SHARDS * HALF
    turned = []
    for part in parts:
        high, low = split(part.reshape(rows, ROWS))
        first = dot(sh[...], high) + dot(sl[...], high)
        if not exact:
            first = first + dot(sh[...], low)
        real, imag = [first[i * rows : (i + 1) * rows].reshape(SHARDS, HALF, ROWS) for i in (0, 1)]
        turned.append(
            jnp.concatenate(
                [
                    (real * twist[0] + imag * twist[1]).reshape(rows, ROWS),
                    (imag * twist[0] - real * twist[1]).reshape(rows, ROWS),
                ],
                axis=1,
            )
        )
    high, low = split(jnp.concatenate(turned, axis=0))
    return dot(high, th[...]) + dot(low, th[...]) + dot(high, tl[...])


def inverse(real, imag, sh, sl, vh, vl, th, tl, twist):
    high, low = split(jnp.concatenate([real, -imag], axis=1))
    back = dot(high, th[...]) + dot(low, th[...]) + dot(high, tl[...])
    rows = SHARDS * HALF
    outs = []
    for g in range(2):
        real, minus = [
            back[g * rows : (g + 1) * rows, i * ROWS : (i + 1) * ROWS].reshape(SHARDS, HALF, ROWS)
            for i in (0, 1)
        ]
        high, low = split(
            jnp.concatenate(
                [
                    (real * twist[0] + minus * twist[1]).reshape(rows, ROWS),
                    (real * twist[1] - minus * twist[0]).reshape(rows, ROWS),
                ],
                axis=0,
            )
        )
        out = dot(vh[...], high) + dot(vh[...], low) + dot(vl[...], high)
        outs.append(out.reshape(SHARDS, HALF, ROWS))
    return outs


def turned_lanes(part, amount):
    flat = pltpu.roll(part.reshape(SHARDS * HALF, ROWS), amount, axis=1)
    return flat.reshape(SHARDS, HALF, ROWS)


def lane(part):
    return lax.broadcasted_iota(jnp.int32, part.shape, part.ndim - 1)


def earlier(part, j):
    turned = turned_lanes(part, j)
    before = jnp.concatenate([jnp.zeros((1, HALF, ROWS), F32), turned[:-1]], axis=0)
    return jnp.where(lane(part) < j, before, turned)


def later(part, j):
    turned = turned_lanes(part, ROWS - j)
    behind = jnp.concatenate([turned[1:], jnp.zeros((1, HALF, ROWS), F32)], axis=0)
    return jnp.where(lane(part) >= ROWS - j, behind, turned)


def channels(moved, i, g):
    part = moved[:, i] if i is not None else moved[...]
    return part.astype(F32).reshape(SHARDS, 2, HALF, ROWS)[:, g]


def conv_kernel(*refs):
    moved, lines, *table, spec_mix, spec_fil, y_full, queries, keys, values = refs
    for g in range(2):
        group = slice(HALF * g, HALF * (g + 1))
        for s in range(3):
            part = channels(moved, s, g)
            total = lines[3 * s, group] * part
            for j in (1, 2):
                total = total + lines[3 * s + j, group] * earlier(part, j)
            (queries, keys, values)[s][g] = total
    for out in (queries, keys, values):
        out.start()
    mix = forward([keys[g] * values[g] for g in range(2)], False, *table)
    fil = forward([channels(moved, 3, g) for g in range(2)], True, *table)
    spec_mix[...] = mix
    spec_mix.start()
    spec_fil[...] = fil
    spec_fil.start()
    mix_re, mix_im = mix[:, :ROWS], mix[:, ROWS:]
    fil_re, fil_im = fil[:, :ROWS], fil[:, ROWS:]
    conv_y = inverse(
        mix_re * fil_re - mix_im * fil_im, mix_re * fil_im + mix_im * fil_re, *table
    )
    for g in range(2):
        group = slice(HALF * g, HALF * (g + 1))
        y_full[g] = conv_y[g] + lines[9, group] * (keys[g] * values[g])


def grad_kernel(*refs):
    grad_moved, queries, *table, spec_mix, spec_fil, y_full, lines, moved, keys, values, out, kept = (
        refs
    )
    grad_y = [channels(grad_moved, None, g) * queries[g] for g in range(2)]
    grad = forward(grad_y, False, *table)
    grad_re, grad_im = grad[:, :ROWS], grad[:, ROWS:]

    def correlate(spec):
        re, im = spec[:, :ROWS], spec[:, ROWS:]
        return inverse(grad_re * re + grad_im * im, grad_im * re - grad_re * im, *table)

    def put(i, parts):
        both = jnp.concatenate(parts, axis=1).astype(BF16)
        out[:, 32 * i : 32 * i + 16, :] = both[:, :, :128]
        out[:, 32 * i + 16 : 32 * i + 32, :] = both[:, :, 128:]

    put(3, correlate(spec_mix))
    conv_back = correlate(spec_fil)
    place = lax.broadcasted_iota(jnp.int32, (HALF, 128), 1)
    sums = jnp.zeros((HALF, 128), F32)
    for s in range(3):
        for g in range(2):
            group = slice(HALF * g, HALF * (g + 1))
            if s == 0:
                part = channels(grad_moved, None, g) * y_full[g]
            else:
                part = (conv_back[g] + lines[9, group] * grad_y[g]) * (values, keys)[s - 1][g]
            stream = channels(moved, s, g)
            total = jnp.zeros_like(part)
            for j in range(3):
                ahead = later(part, j) if j else part
                total = total + lines[3 * s + j, group] * ahead
                term = jnp.sum(jnp.sum(ahead * stream, axis=0), axis=1, keepdims=True)
                sums = jnp.where(place == 10 * g + 3 * s + j, term, sums)
            kept[g] = total
        put(s, [kept[0], kept[1]])
    for g in range(2):
        term = jnp.sum(
            jnp.sum(grad_y[g] * (keys[g] * values[g]), axis=0), axis=1, keepdims=True
        )
        sums = jnp.where(place == 10 * g + 9, term, sums)
    high = sums.astype(BF16).astype(F32)
    sums = high + pltpu.roll(sums - high, 64, axis=1)
    out[:, 128:136, :] = jnp.broadcast_to(sums[None], (SHARDS, HALF, 128)).astype(BF16)


def pack_kernel(queries, keys, values, long_filter, send):
    for s, stream in enumerate((queries, keys, values, long_filter)):
        send[:, s] = stream[...].astype(F32).T.reshape(SHARDS, GROUP, ROWS).astype(BF16)


def unpack_kernel(moved, d_queries, d_keys, d_values, d_long, d_short, d_skip):
    for i, out in enumerate((d_queries, d_keys, d_values, d_long)):
        for half in range(2):
            start = 32 * i + 16 * half
            part = moved[:, start : start + 16, :].astype(F32).reshape(WIDTH, 128)
            out[128 * half : 128 * (half + 1), :] = part.T.astype(out.dtype)
    sums = moved[:, 128:136, :].astype(F32).reshape(SHARDS * HALF, 128).T
    source = lax.broadcasted_iota(jnp.int32, (SHARDS * HALF, WIDTH), 0)
    target = lax.broadcasted_iota(jnp.int32, (SHARDS * HALF, WIDTH), 1)
    totals = jnp.zeros((10, WIDTH), F32)
    for g in range(2):
        aim = source + (source // HALF) * HALF + HALF * g
        place = (target == aim).astype(F32).astype(BF16)
        spread = dot(sums.astype(BF16), place)
        totals = totals + spread[10 * g : 10 * g + 10] + spread[64 + 10 * g : 64 + 10 * g + 10]
    for s in range(3):
        d_short[s] = totals[3 * s : 3 * s + 3]
    d_skip[...] = totals[9:10]


def project_kernel(count, at, first, last, *refs):
    blocks, (w_out, order, *rest) = refs[:count], refs[count:]
    held, own, arrived = rest[-3:]
    depth = blocks[0].shape[1]
    if first:
        block = Arriving(blocks[0], own, own, arrived.at[count])
        block.start()
        blocks = [block, *blocks[1:]]
    slices = []
    for i in range(count):
        columns = pl.ds(pl.multiple_of(order[at + i] * depth, depth), depth)
        slices.append(Arriving(w_out.at[:, columns], held.at[i], held.at[i], arrived.at[i]))
        slices[-1].start()
    total = jnp.zeros((WIDTH, ROWS), F32) if first else rest[0][...]
    for i in range(count):
        total = total + lax.dot_general(
            slices[i][...], blocks[i][...], (((1,), (1,)), ((), ())), preferred_element_type=F32
        )
    out = rest[0 if first else 1]
    out[...] = total.astype(BF16).reshape(SHARDS, GROUP, ROWS) if last else total


def project(blocks, at, w_out, order, before=None, last=False):
    count = len(blocks)
    depth = blocks[0].shape[1]
    first = before is None
    vmem = pl.BlockSpec(memory_space=pltpu.VMEM)
    anywhere = pl.BlockSpec(memory_space=pl.ANY)
    specs = [anywhere if first and i == 0 else vmem for i in range(count)]
    specs += [anywhere, pl.BlockSpec(memory_space=pltpu.SMEM)] + [vmem] * (not first)
    blocks = [in_hbm(b) if first and i == 0 else in_vmem(b) for i, b in enumerate(blocks)]
    return pl.pallas_call(
        functools.partial(project_kernel, count, at, first, last),
        out_shape=shape((SHARDS, GROUP, ROWS), BF16) if last else shape((WIDTH, ROWS)),
        in_specs=specs,
        out_specs=vmem,
        scratch_shapes=[
            pltpu.VMEM((count, WIDTH, depth), BF16),
            pltpu.VMEM((ROWS, depth), BF16),
            pltpu.SemaphoreType.DMA((count + 1,)),
        ],
        compiler_params=pltpu.CompilerParams(vmem_limit_bytes=12 * MIB),
        cost_estimate=pl.CostEstimate(
            flops=2 * count * ROWS * depth * WIDTH,
            bytes_accessed=2 * count * WIDTH * depth,
            transcendentals=0,
        ),
        name="project",
    )(*blocks, in_hbm(w_out), order, *([] if first else [in_vmem(before)]))


def in_vmem(array):
    return pltpu.with_memory_space_constraint(array, pltpu.VMEM)


def in_hbm(array):
    return pltpu.with_memory_space_constraint(array, pltpu.HBM)


class Moving:
    def __init__(self, source, target, held, done):
        self.copy, self.held = pltpu.make_async_copy(source, target, done), held
        self.started = self.ended = False
        self.dtype = held.dtype

    def start(self):
        if not self.started:
            self.copy.start()
            self.started = True

    def wait(self):
        self.start()
        if not self.ended:
            self.copy.wait()
            self.ended = True


class Arriving(Moving):
    behind = ()

    def __getitem__(self, index):
        self.wait()
        for array in self.behind:
            array.start()
        return self.held[index]


class Leaving(Moving):
    def __getitem__(self, index):
        return self.held[index]

    def __setitem__(self, index, value):
        self.held[index] = value


def staged_kernel(kernel, count, outs, urgent, *refs):
    sources, targets, refs = refs[:count], refs[count : count + outs], refs[count + outs :]
    held, built = refs[:count], refs[count:]
    built, (*scratch, arrived, sent) = built[:outs], built[outs:]
    arriving = [Arriving(sources[i], held[i], held[i], arrived.at[i]) for i in range(count)]
    leaving = [Leaving(built[i], targets[i], built[i], sent.at[i]) for i in range(outs)]
    for array in arriving[:urgent]:
        array.start()
    arriving[urgent - 1].behind = arriving[urgent:]
    kernel(*arriving, *leaving, *scratch)
    for array in (*arriving, *leaving):
        array.start()
    for array in (*arriving, *leaving):
        array.wait()


def call(
    kernel, out_shape, *args, scratch=(), name, limit=12, flops=0, moved=4 * MIB, urgent=None
):
    count, outs = len(args), len(out_shape)
    anywhere = pl.BlockSpec(memory_space=pl.ANY)
    return pl.pallas_call(
        functools.partial(staged_kernel, kernel, count, outs, urgent or count),
        out_shape=out_shape,
        in_specs=[anywhere] * count,
        out_specs=tuple([anywhere] * outs),
        scratch_shapes=(
            *[pltpu.VMEM(arg.shape, arg.dtype) for arg in args],
            *[pltpu.VMEM(out.shape, out.dtype) for out in out_shape],
            *scratch,
            pltpu.SemaphoreType.DMA((count,)),
            pltpu.SemaphoreType.DMA((outs,)),
        ),
        compiler_params=pltpu.CompilerParams(vmem_limit_bytes=limit * MIB),
        cost_estimate=pl.CostEstimate(flops=flops, bytes_accessed=moved, transcendentals=0),
        name=name,
    )(*args)


def exchange(blocks):
    return lax.all_to_all(blocks, CTX, split_axis=0, concat_axis=0, tiled=True)


def shape(dims, dtype=F32):
    return jax.ShapeDtypeStruct(dims, dtype)


def gathered_product(d_out, w_out):
    x_size = lax.axis_size("x")
    x, core = lax.axis_index("x"), lax.axis_index("core")
    near, far = (x + 2 * core - 1) % x_size, (x + 2) % x_size
    other_near = (x + 1 - 2 * core) % x_size
    order = jnp.stack(
        [
            2 * x + core, 2 * x + 1 - core,
            2 * near + core, 2 * other_near + 1 - core,
            2 * near + 1 - core, 2 * other_near + core,
            2 * far + core, 2 * far + 1 - core,
        ]
    ).astype(jnp.int32)
    first, sibling = ahead(d_out), swap(d_out)
    total = project([d_out, sibling], 0, w_out, order)
    second = ahead(sibling)
    third = ahead(first)
    first_other = swap(first)
    second, total = lax.optimization_barrier((second, total))
    second_other = swap(second)
    total = project([first, first_other], 2, w_out, order, total)
    third, total = lax.optimization_barrier((third, total))
    third_other = swap(third)
    total = project([second, second_other], 4, w_out, order, total)
    return project([third, third_other], 6, w_out, order, total, last=True)


def swap(block):
    return lax.ppermute(block, CH, [(i, i ^ 1) for i in range(2 * lax.axis_size("x"))])


def ahead(block):
    size = lax.axis_size("x")
    route = [(2 * i + c, 2 * ((i + 1 - 2 * c) % size) + c) for i in range(size) for c in range(2)]
    return lax.ppermute(block, CH, route)


def per_device(queries, keys, values, long_filter, short, skip, w_out, d_out):
    (send,) = call(
        pack_kernel,
        (shape((SHARDS, 4, GROUP, ROWS), BF16),),
        *[in_hbm(stream) for stream in (queries, keys, values, long_filter)],
        name="pack",
    )
    moved = in_hbm(exchange(send))
    mine = lax.axis_index(CTX) * GROUP
    lines = jnp.concatenate([short.reshape(9, WIDTH), skip[None]], axis=0)
    lines = lax.dynamic_slice(lines, (0, mine), (10, GROUP))
    lines = jnp.broadcast_to(lines[:, :, None], (10, GROUP, ROWS))
    table = [in_hbm(jnp.asarray(array)) for array in tables()]
    grad_moved = exchange(gathered_product(d_out, w_out))
    spec = pltpu.HBM((2 * SHARDS * HALF, 2 * ROWS), F32)
    part = pltpu.HBM((2, SHARDS, HALF, ROWS), F32)
    transform = 2 * 600 * MIB
    kept = call(
        conv_kernel,
        (spec, spec, part, part, part, part),
        moved, lines, *table,
        name="conv", limit=40, flops=3 * transform, urgent=2,
    )
    spec_mix, spec_fil, y_full, *filtered = [in_hbm(array) for array in kept]
    (back,) = call(
        grad_kernel,
        (shape((SHARDS, 136, 128), BF16),),
        grad_moved, filtered[0], *table, spec_mix, spec_fil, y_full, lines, moved, *filtered[1:],
        scratch=(pltpu.VMEM((2, SHARDS, HALF, ROWS), F32),),
        name="grad_conv", limit=40, flops=3 * transform, urgent=2,
    )
    stream = shape((ROWS, WIDTH), BF16)
    *grads, d_short, d_skip = call(
        unpack_kernel,
        (stream, stream, stream, shape((ROWS, WIDTH)), shape((3, 3, WIDTH)), shape((1, WIDTH))),
        exchange(back),
        name="unpack", limit=16,
    )
    return *grads, d_short, d_skip[0]


def solution(mesh):
    fine_mesh = Mesh(mesh.devices.reshape(8, 4, 4, 2), ("z", "y", "x", "core"))
    block = P(CTX, CH)
    in_specs = (block, block, block, block, P(None, None, CH), P(CH), P(CH, None), block)
    out_specs = (block, block, block, block, P(None, None, CH), P(CH))
    return jax.shard_map(
        per_device, mesh=fine_mesh, in_specs=in_specs, out_specs=out_specs, check_vma=False
    )
```
